32 devices in a mesh: ctx: 4 (over z), head: 4 (over y, x), section: 2 (over core).
Axes of the slice: x: 2, y: 2, z: 4, core: 2. Of those that a mesh axis runs over, the one named last changes fastest.
Arguments:
- queries: bfloat16 [2, 512, 16384], P('section', 'ctx', 'head')
- keys: bfloat16 [2, 512, 1024], P('section', 'ctx', 'head')
- values: bfloat16 [2, 512, 1024], P('section', 'ctx', 'head'), may hold values from -6 to 6
- order: int32 [512], replicated, may hold values from 0 to 511, as said below
- doc_lengths: int32 [16], replicated, may hold values from 1 to 256, 512 in all
Outputs:
- handed: bfloat16 [2, 512, 16384], P('section', ('ctx', 'head'))
The draws below stay inside these ranges and needn't reach their ends.
Inputs may be any that keep to these rules, and one draw needn't show every extreme that they name: The stored tokens of ctx index c are two aligned runs of 64 pack positions, run j and run 2 * 4 - 1 - j, each in rising order, j a permutation of the indices drawn from the seed.
All inputs are finite; a program needn't handle non-finite values.
Results may differ from the reference program's by a relative error of at most 0.0075.
Values may be sent and summed in bfloat16 or wider, within the bound.
No kernel may reach another device: no remote copies, remote signals or barrier semaphores. Data moves between devices by JAX's collectives and lax.ppermute only.
A program may use at most 64 MiB of HBM per device.

```python
import math
import jax
import jax.numpy as jnp
import numpy as np
from jax import lax

HEADS = 128
KV_HEADS = 8
HD = 128
TOK_DEV = 128
NDOC = 16
TOKENS = 512
LAYERS = 2


def key_table(key):
    return jnp.clip(jax.random.normal(jax.random.fold_in(key, 7), (LAYERS, TOKENS, KV_HEADS * HD), jnp.float32), -4.0, 4.0)


def draw_keys(key, part):
    return key_table(key).astype(jnp.bfloat16)


def draw_queries(key, part):
    base = jnp.clip(jax.random.normal(jax.random.fold_in(key, 11), (LAYERS, TOKENS, HEADS * HD), jnp.float32), -4.0, 4.0)
    return base.astype(jnp.bfloat16)


def draw_order(key, part):
    runs = TOKENS // TOK_DEV
    half = TOK_DEV // 2
    pairs = jax.random.permutation(key, runs).astype(jnp.int32)
    index = jnp.arange(TOKENS, dtype=jnp.int32)
    shard = index // TOK_DEV
    within = index % TOK_DEV
    chosen = pairs[shard]
    first = chosen * half + within
    second = (2 * runs - 1 - chosen) * half + within - half
    return jnp.where(within < half, first, second).astype(jnp.int32)


def steps_of(own_key, dims, shards, smallest, top_value):
    def one(axis_at, blocks):
        heights = jax.random.uniform(jax.random.fold_in(jax.random.fold_in(own_key, 6), axis_at), (blocks,), jnp.float32, smallest / len(shards), top_value / len(shards))
        return jnp.repeat(jnp.exp(heights), dims[axis_at] // blocks).reshape((-1,) + (1,) * (len(dims) - axis_at - 1))

    loudness = one(*shards[0])
    for cut in shards[1:]:
        loudness = loudness * one(*cut)
    return loudness


def length_profile(number_of, total, limit, lean):
    weights = [(1 << 20) // math.isqrt(standing ** lean) + 1 for standing in range(2, number_of + 1)]
    spare, given = total - limit - (number_of - 1), [1] * (number_of - 1)
    while spare > 0:
        free = [i for i in range(number_of - 1) if given[i] < limit]
        whole, left = sum([weights[i] for i in free]), spare
        for i in free:
            extra = min(limit - given[i], max(1, left * weights[i] // whole), spare)
            given[i] = given[i] + extra
            spare = spare - extra
    return np.array([limit] + given)


def uneven(rng, amount, total, most, slope):
    if amount == 2:
        one = jax.random.randint(rng, (), max(1, total - most), min(most, total - 1) + 1)
        return jnp.stack([one, total - one])
    tallies = jnp.asarray(length_profile(amount, total, most, slope), jnp.int32)
    twos = (amount - 1) // 2
    donor, taker = tallies[1:1 + 2 * twos:2], tallies[2:2 + 2 * twos:2]
    margin = jnp.minimum(donor - 1, most - taker)
    shifted = jax.random.randint(jax.random.fold_in(rng, 1), (twos,), 0, 1 << 20) % (margin + 1)
    tallies = tallies.at[1:1 + 2 * twos:2].set(donor - shifted).at[2:2 + 2 * twos:2].set(taker + shifted)
    return tallies[jax.random.permutation(jax.random.fold_in(rng, 2), amount)]


def centred(key, extent, scale, reach, shards=(), held_as=jnp.bfloat16):
    result = scale * jax.random.normal(key, extent, jnp.float32)
    if shards:
        result = result * steps_of(key, extent, shards, -0.22, 0.18)
    return jnp.clip(result, -reach, reach).astype(held_as)


def setup_inputs(seed: int = 0) -> dict:
    splits = jax.random.split(jax.random.key(seed), 6)
    return {
        "queries": draw_queries(jax.random.fold_in(splits[5], 71), 0),
        "keys": draw_keys(jax.random.fold_in(splits[5], 71), 0),
        "values": centred(splits[2], (LAYERS, TOKENS, KV_HEADS * HD), 1.0, 6.0, ((0, 2), (1, 4), (2, 4))),
        "order": draw_order(jax.random.fold_in(splits[5], 71), 0),
        "doc_lengths": uneven(splits[4], NDOC, TOKENS, TOKENS // 2, 2).astype(jnp.int32),
    }


def reference(queries, keys, values, order, doc_lengths):
    starts = jnp.cumsum(doc_lengths) - doc_lengths
    doc = jnp.sum((order[:, None] >= starts[None, :]).astype(jnp.int32), axis=1) - 1
    allowed = (doc[:, None] == doc[None, :]) & (order[None, :] <= order[:, None])
    group = HEADS // KV_HEADS
    scale = 1.0 / (HD ** 0.5)
    q_all = queries.reshape(LAYERS, TOKENS, KV_HEADS, group, HD)
    k_all = keys.reshape(LAYERS, TOKENS, KV_HEADS, HD)
    v_all = values.reshape(LAYERS, TOKENS, KV_HEADS, HD)

    def one_group(index):
        layer = index // KV_HEADS
        kvh = index % KV_HEADS
        qg = q_all[layer][:, kvh].astype(jnp.float32)
        kg = k_all[layer][:, kvh].astype(jnp.float32)
        vg = v_all[layer][:, kvh].astype(jnp.float32)
        score = jnp.einsum('tgd,sd->gts', qg, kg) * scale
        score = jnp.where(allowed[None], score, -1e30)
        top = jnp.max(score, axis=2, keepdims=True)
        weight = jnp.where(allowed[None], jnp.exp(score - top), 0.0)
        total = jnp.sum(weight, axis=2, keepdims=True)
        weight_b = weight.astype(jnp.bfloat16).astype(jnp.float32)
        numer = jnp.einsum('gts,sd->gtd', weight_b, vg)
        return jnp.transpose(numer / total, (1, 0, 2)).astype(jnp.bfloat16)

    attn = lax.map(one_group, jnp.arange(LAYERS * KV_HEADS, dtype=jnp.int32))
    attn = attn.reshape(LAYERS, KV_HEADS, TOKENS, group, HD)
    attn = jnp.transpose(attn, (0, 2, 1, 3, 4)).reshape(LAYERS, TOKENS, HEADS * HD)
    return jnp.roll(attn, 1, axis=0)
```

```python
import functools

import jax
import jax.numpy as jnp
from jax import lax
from jax.experimental import pallas as pl
from jax.experimental.pallas import tpu as pltpu
from jax.sharding import PartitionSpec as P

HD = 128
LOG2E = 1.4426950408889634
VMEM = pltpu.VMEM
VMEM_LIMIT = 48 * 1024 * 1024
BLOCK = 8


def bias_kernel(lengths, order, *refs):
    bias = refs[-1]
    shards, rows = order.shape
    c = lax.axis_index("ctx")
    pos = order[pl.ds(c, 1), :]
    lo = jnp.zeros_like(pos)
    start = jnp.int32(0)
    for n in range(lengths.shape[0]):
        lo = jnp.where(pos >= start, start, lo)
        start = start + lengths[n]
    square = (rows, rows)
    pos_rows = jnp.transpose(jnp.broadcast_to(pos.astype(jnp.float32), square))
    lo_rows = jnp.transpose(jnp.broadcast_to(lo.astype(jnp.float32), square))

    for step in range(shards):
        key_pos = order[pl.ds(jnp.bitwise_xor(c, step), 1), :].astype(jnp.float32)
        seen = (key_pos >= lo_rows) & (key_pos <= pos_rows)
        bias[:, step * rows : (step + 1) * rows] = jnp.where(seen, 0.0, -jnp.inf)


def attend_kernel(scale, slots, pieces, q, bias, *refs):
    outs = refs[-len(slots) :]
    part, width = outs[0].shape
    heads = width // HD
    me = lax.axis_index("head")
    for index, group in enumerate(sorted({group for _, group in slots})):
        kvs = refs[index * pieces : (index + 1) * pieces]
        kvs = [kv[group] if len(kv.shape) == 3 else kv[...] for kv in kvs]
        keys = jnp.concatenate([kv[:, :HD] for kv in kvs], axis=0)
        vals = jnp.concatenate([kv[:, HD:] for kv in kvs], axis=0)
        vals = jnp.concatenate([vals, jnp.ones_like(vals)], axis=1)
        for d, out in [(d, out) for (d, g), out in zip(slots, outs) if g == group]:
            rows = pl.ds(pl.multiple_of(jnp.bitwise_xor(me, d) * part, part), part)
            seen = bias[rows, :][None]
            for first in range(0, heads, BLOCK):
                block = [slice(j * HD, (j + 1) * HD) for j in range(first, min(first + BLOCK, heads))]
                shift = group * width
                stacked = jnp.concatenate(
                    [q[0, rows, shift + col.start : shift + col.stop] for col in block], axis=0
                )
                score = lax.dot_general(
                    stacked, keys, (((1,), (1,)), ((), ())), preferred_element_type=jnp.float32
                )
                score = score.reshape(len(block), part, -1) + seen
                top = jnp.max(score, axis=2, keepdims=True)
                weight = jnp.exp2((score - top) * scale).astype(jnp.bfloat16)
                both = jnp.dot(
                    weight.reshape(len(block) * part, -1), vals, preferred_element_type=jnp.float32
                )
                attn = (both[:, :HD] / both[:, HD:]).astype(jnp.bfloat16)
                for j, col in enumerate(block):
                    out[:, col] = attn[j * part : (j + 1) * part]


def place_kernel(slots, groups, *refs):
    pieces, out, sem = refs[: len(slots)], refs[-2], refs[-1]
    width = pieces[0].shape[1]
    me = lax.axis_index("head")
    copies = []
    for index, (d, g) in enumerate(slots):
        at = pl.multiple_of((jnp.bitwise_xor(me, d) * groups + g) * width, width)
        copies.append(
            pltpu.make_async_copy(pieces[index], out.at[0, :, pl.ds(at, width)], sem.at[index])
        )
    for copy in copies:
        copy.start()
    for copy in copies:
        copy.wait()


def local(queries, keys, values, order, doc_lengths):
    rows = queries.shape[1]
    groups = keys.shape[2] // HD
    width = queries.shape[2] // groups
    shards = lax.axis_size("ctx")
    heads = lax.axis_size("head")
    sections = lax.axis_size("section")
    part = rows // heads
    smem = pl.BlockSpec(memory_space=pltpu.SMEM)
    vmem = pl.BlockSpec(memory_space=VMEM)
    anywhere = pl.BlockSpec(memory_space=pl.ANY)
    params = pltpu.CompilerParams(vmem_limit_bytes=VMEM_LIMIT)
    turn = sorted(range(heads), key=lambda d: (-bin(d).count("1"), d))

    def handed(value, step):
        pairs = [
            (c * sections + s, (c ^ step) * sections + (s + 1) % sections)
            for c in range(shards)
            for s in range(sections)
        ]
        return lax.ppermute(value, ("ctx", "section"), pairs)

    def passed(value, step):
        return lax.ppermute(value, "ctx", [(c, c ^ step) for c in range(shards)])

    def after(value, *others):
        return lax.optimization_barrier((value, *others))[0]

    rows_q = handed(queries, 0)
    bias = pl.pallas_call(
        bias_kernel,
        out_shape=jax.ShapeDtypeStruct((rows, rows * shards), jnp.float32),
        in_specs=[smem, vmem],
        out_specs=vmem,
        compiler_params=params,
        name="bias",
    )(doc_lengths, order.reshape(shards, rows))

    packed = [
        jnp.concatenate([kv[0, :, g * HD : (g + 1) * HD] for kv in (keys, values)], axis=1)
        for g in range(groups)
    ]
    stacked = jnp.stack(packed)
    step = shards // 2
    blocks = {step: [handed(block, step) for block in packed]}
    own = handed(after(stacked, bias), 0)
    while step > 1:
        step //= 2
        for other in sorted(blocks):
            blocks[other ^ step] = [passed(after(block, bias), step) for block in blocks[other]]
        blocks[step] = [handed(after(stacked, bias), step)]
    kvs = [
        [own] + [blocks[step][g % len(blocks[step])] for step in range(1, shards)]
        for g in range(groups)
    ]

    def attend(slots, *others):
        needed = [block for g in sorted({g for _, g in slots}) for block in kvs[g]]
        return pl.pallas_call(
            functools.partial(attend_kernel, LOG2E / HD**0.5, slots, shards),
            out_shape=[jax.ShapeDtypeStruct((part, width), jnp.bfloat16)] * len(slots),
            in_specs=[vmem] * (2 + len(needed)) + [anywhere] * len(others),
            out_specs=[vmem] * len(slots),
            compiler_params=params,
            cost_estimate=pl.CostEstimate(
                flops=4 * part * width * rows * shards * len(slots),
                bytes_accessed=4 * part * width * len(slots),
                transcendentals=rows * shards * part * width // HD * len(slots),
            ),
            name="attend",
        )(rows_q, bias, *needed, *others)

    arrived = {}
    last = []
    for g in range(groups):
        parts = ((3,), (1, 2)) if g + 1 < groups else ((3, 1, 2),)
        for index, partners in enumerate(parts):
            for d in [(3,)][index] if g else ():
                last.append(arrived[d, g - 1])
            slots = [(d, g) for d in partners]
            pieces = attend(slots, *last)
            last = [pieces[-1]]
            for (d, _), piece in zip(slots, pieces):
                arrived[d, g] = lax.ppermute(piece, "head", [(h, h ^ d) for h in range(heads)])
    slots = [(0, g) for g in range(groups)]
    for slot, piece in zip(slots, attend(slots, *last)):
        arrived[slot] = piece

    final = groups - 1
    out = []
    for slots in [[(d, g) for g in range(final) for d in turn[:-1]] + [(0, g) for g in range(groups)], [(turn[0], final)], [(d, final) for d in turn[1:-1]]]:
        out = [
            pl.pallas_call(
                functools.partial(place_kernel, slots, groups),
                out_shape=jax.ShapeDtypeStruct((1, part, heads * groups * width), jnp.bfloat16),
                in_specs=[anywhere] * (len(slots) + len(out)),
                out_specs=anywhere,
                scratch_shapes=[pltpu.SemaphoreType.DMA((len(slots),))],
                input_output_aliases={len(slots): 0} if out else {},
                compiler_params=params,
                name="place",
            )(*[arrived[slot] for slot in slots], *out)
        ]
    return out[0]


def solution(mesh):
    in_specs = (
        P("section", "ctx", "head"),
        P("section", "ctx", "head"),
        P("section", "ctx", "head"),
        P(),
        P(),
    )
    out_specs = P("section", ("ctx", "head"), None)
    return jax.shard_map(local, mesh=mesh, in_specs=in_specs, out_specs=out_specs, check_vma=False)
```

```python
import functools

import jax
import jax.numpy as jnp
from jax import lax
from jax.experimental import pallas as pl
from jax.experimental.pallas import tpu as pltpu
from jax.sharding import PartitionSpec as P

HD = 128
LOG2E = 1.4426950408889634
VMEM = pltpu.VMEM
VMEM_LIMIT = 48 * 1024 * 1024
BLOCK = 8


def bias_kernel(lengths, order, *refs):
    bias = refs[-1]
    shards, rows = order.shape
    c = lax.axis_index("ctx")
    pos = order[pl.ds(c, 1), :]
    lo = jnp.zeros_like(pos)
    start = jnp.int32(0)
    for n in range(lengths.shape[0]):
        lo = jnp.where(pos >= start, start, lo)
        start = start + lengths[n]
    square = (rows, rows)
    pos_rows = jnp.transpose(jnp.broadcast_to(pos.astype(jnp.float32), square))
    lo_rows = jnp.transpose(jnp.broadcast_to(lo.astype(jnp.float32), square))

    for step in range(shards):
        key_pos = order[pl.ds(jnp.bitwise_xor(c, step), 1), :].astype(jnp.float32)
        seen = (key_pos >= lo_rows) & (key_pos <= pos_rows)
        bias[:, step * rows : (step + 1) * rows] = jnp.where(seen, 0.0, -jnp.inf)


def attend_kernel(scale, slots, pieces, q, bias, *refs):
    outs = refs[-len(slots) :]
    part, width = outs[0].shape
    heads = width // HD
    me = lax.axis_index("head")
    for index, group in enumerate(sorted({group for _, group in slots})):
        kvs = refs[index * pieces : (index + 1) * pieces]
        kvs = [kv[group] if len(kv.shape) == 3 else kv[...] for kv in kvs]
        keys = jnp.concatenate([kv[:, :HD] for kv in kvs], axis=0)
        vals = jnp.concatenate([kv[:, HD:] for kv in kvs], axis=0)
        vals = jnp.concatenate([vals, jnp.ones_like(vals)], axis=1)
        for d, out in [(d, out) for (d, g), out in zip(slots, outs) if g == group]:
            rows = pl.ds(pl.multiple_of(jnp.bitwise_xor(me, d) * part, part), part)
            seen = bias[rows, :][None]
            for first in range(0, heads, BLOCK):
                block = [slice(j * HD, (j + 1) * HD) for j in range(first, min(first + BLOCK, heads))]
                shift = group * width
                stacked = jnp.concatenate(
                    [q[0, rows, shift + col.start : shift + col.stop] for col in block], axis=0
                )
                score = lax.dot_general(
                    stacked, keys, (((1,), (1,)), ((), ())), preferred_element_type=jnp.float32
                )
                score = score.reshape(len(block), part, -1) + seen
                top = jnp.max(score, axis=2, keepdims=True)
                weight = jnp.exp2((score - top) * scale).astype(jnp.bfloat16)
                both = jnp.dot(
                    weight.reshape(len(block) * part, -1), vals, preferred_element_type=jnp.float32
                )
                attn = (both[:, :HD] / both[:, HD:]).astype(jnp.bfloat16)
                for j, col in enumerate(block):
                    out[:, col] = attn[j * part : (j + 1) * part]


def place_kernel(slots, groups, *refs):
    pieces, out, sem = refs[: len(slots)], refs[-2], refs[-1]
    width = pieces[0].shape[1]
    me = lax.axis_index("head")
    copies = []
    for index, (d, g) in enumerate(slots):
        at = pl.multiple_of((jnp.bitwise_xor(me, d) * groups + g) * width, width)
        copies.append(
            pltpu.make_async_copy(pieces[index], out.at[0, :, pl.ds(at, width)], sem.at[index])
        )
    for copy in copies:
        copy.start()
    for copy in copies:
        copy.wait()


def local(queries, keys, values, order, doc_lengths):
    rows = queries.shape[1]
    groups = keys.shape[2] // HD
    width = queries.shape[2] // groups
    shards = lax.axis_size("ctx")
    heads = lax.axis_size("head")
    sections = lax.axis_size("section")
    part = rows // heads
    smem = pl.BlockSpec(memory_space=pltpu.SMEM)
    vmem = pl.BlockSpec(memory_space=VMEM)
    anywhere = pl.BlockSpec(memory_space=pl.ANY)
    params = pltpu.CompilerParams(vmem_limit_bytes=VMEM_LIMIT)
    turn = sorted(range(heads), key=lambda d: (-bin(d).count("1"), d))

    def handed(value, step):
        pairs = [
            (c * sections + s, (c ^ step) * sections + (s + 1) % sections)
            for c in range(shards)
            for s in range(sections)
        ]
        return lax.ppermute(value, ("ctx", "section"), pairs)

    def passed(value, step):
        return lax.ppermute(value, "ctx", [(c, c ^ step) for c in range(shards)])

    def after(value, *others):
        return lax.optimization_barrier((value, *others))[0]

    rows_q = handed(queries, 0)
    bias = pl.pallas_call(
        bias_kernel,
        out_shape=jax.ShapeDtypeStruct((rows, rows * shards), jnp.float32),
        in_specs=[smem, vmem],
        out_specs=vmem,
        compiler_params=params,
        name="bias",
    )(doc_lengths, order.reshape(shards, rows))

    packed = [
        jnp.concatenate([kv[0, :, g * HD : (g + 1) * HD] for kv in (keys, values)], axis=1)
        for g in range(groups)
    ]
    stacked = jnp.stack(packed)
    step = shards // 2
    blocks = {step: [handed(block, step) for block in packed]}
    own = handed(after(stacked, bias), 0)
    while step > 1:
        step //= 2
        for other in sorted(blocks):
            blocks[other ^ step] = [passed(after(block, bias), step) for block in blocks[other]]
        blocks[step] = [handed(after(stacked, bias), step)]
    kvs = [
        [own] + [blocks[step][g % len(blocks[step])] for step in range(1, shards)]
        for g in range(groups)
    ]

    def attend(slots, *others):
        needed = [block for g in sorted({g for _, g in slots}) for block in kvs[g]]
        return pl.pallas_call(
            functools.partial(attend_kernel, LOG2E / HD**0.5, slots, shards),
            out_shape=[jax.ShapeDtypeStruct((part, width), jnp.bfloat16)] * len(slots),
            in_specs=[vmem] * (2 + len(needed)) + [anywhere] * len(others),
            out_specs=[vmem] * len(slots),
            compiler_params=params,
            cost_estimate=pl.CostEstimate(
                flops=16 * part * width * rows * shards * len(slots),
                bytes_accessed=4 * part * width * len(slots),
                transcendentals=rows * shards * part * width // HD * len(slots),
            ),
            name="attend",
        )(rows_q, bias, *needed, *others)

    arrived = {}
    last = []
    for g in range(groups):
        parts = ((3,), (1, 2)) if g + 1 < groups else ((3, 1, 2),)
        for index, partners in enumerate(parts):
            slots = [(d, g) for d in partners]
            pieces = attend(slots, *last)
            last = [pieces[-1]]
            for (d, _), piece in zip(slots, pieces):
                if g and d == 2:
                    piece = after(piece, arrived[1, g - 1])
                arrived[d, g] = lax.ppermute(piece, "head", [(h, h ^ d) for h in range(heads)])
    slots = [(0, g) for g in range(groups)]
    for slot, piece in zip(slots, attend(slots, *last)):
        arrived[slot] = piece

    final = groups - 1
    out = []
    for slots in [[(d, g) for g in range(final) for d in turn[:-1]] + [(0, g) for g in range(groups)], [(turn[0], final)], [(d, final) for d in turn[1:-1]]]:
        out = [
            pl.pallas_call(
                functools.partial(place_kernel, slots, groups),
                out_shape=jax.ShapeDtypeStruct((1, part, heads * groups * width), jnp.bfloat16),
                in_specs=[anywhere] * (len(slots) + len(out)),
                out_specs=anywhere,
                scratch_shapes=[pltpu.SemaphoreType.DMA((len(slots),))],
                input_output_aliases={len(slots): 0} if out else {},
                compiler_params=params,
                name="place",
            )(*[arrived[slot] for slot in slots], *out)
        ]
    return out[0]


def solution(mesh):
    in_specs = (
        P("section", "ctx", "head"),
        P("section", "ctx", "head"),
        P("section", "ctx", "head"),
        P(),
        P(),
    )
    out_specs = P("section", ("ctx", "head"), None)
    return jax.shard_map(local, mesh=mesh, in_specs=in_specs, out_specs=out_specs, check_vma=False)
```

```python
import functools

import jax
import jax.numpy as jnp
from jax import lax
from jax.experimental import pallas as pl
from jax.experimental.pallas import tpu as pltpu
from jax.sharding import PartitionSpec as P

HD = 128
LOG2E = 1.4426950408889634
VMEM = pltpu.VMEM
VMEM_LIMIT = 48 * 1024 * 1024
BLOCK = 8


def bias_kernel(lengths, order, *refs):
    bias = refs[-1]
    shards, rows = order.shape
    c = lax.axis_index("ctx")
    pos = order[pl.ds(c, 1), :]
    lo = jnp.zeros_like(pos)
    start = jnp.int32(0)
    for n in range(lengths.shape[0]):
        lo = jnp.where(pos >= start, start, lo)
        start = start + lengths[n]
    square = (rows, rows)
    pos_rows = jnp.transpose(jnp.broadcast_to(pos.astype(jnp.float32), square))
    lo_rows = jnp.transpose(jnp.broadcast_to(lo.astype(jnp.float32), square))

    for step in range(shards):
        key_pos = order[pl.ds(jnp.bitwise_xor(c, step), 1), :].astype(jnp.float32)
        seen = (key_pos >= lo_rows) & (key_pos <= pos_rows)
        bias[:, step * rows : (step + 1) * rows] = jnp.where(seen, 0.0, -jnp.inf)


def attend_kernel(scale, slots, pieces, q, bias, *refs):
    outs = refs[-len(slots) :]
    part, width = outs[0].shape
    heads = width // HD
    me = lax.axis_index("head")
    for index, group in enumerate(sorted({group for _, group in slots})):
        kvs = refs[index * pieces : (index + 1) * pieces]
        kvs = [kv[group] if len(kv.shape) == 3 else kv[...] for kv in kvs]
        keys = jnp.concatenate([kv[:, :HD] for kv in kvs], axis=0)
        vals = jnp.concatenate([kv[:, HD:] for kv in kvs], axis=0)
        vals = jnp.concatenate([vals, jnp.ones_like(vals)], axis=1)
        for d, out in [(d, out) for (d, g), out in zip(slots, outs) if g == group]:
            rows = pl.ds(pl.multiple_of(jnp.bitwise_xor(me, d) * part, part), part)
            seen = bias[rows, :][None]
            for first in range(0, heads, BLOCK):
                block = [slice(j * HD, (j + 1) * HD) for j in range(first, min(first + BLOCK, heads))]
                shift = group * width
                stacked = jnp.concatenate(
                    [q[0, rows, shift + col.start : shift + col.stop] for col in block], axis=0
                )
                score = lax.dot_general(
                    stacked, keys, (((1,), (1,)), ((), ())), preferred_element_type=jnp.float32
                )
                score = score.reshape(len(block), part, -1) + seen
                top = jnp.max(score, axis=2, keepdims=True)
                weight = jnp.exp2((score - top) * scale).astype(jnp.bfloat16)
                both = jnp.dot(
                    weight.reshape(len(block) * part, -1), vals, preferred_element_type=jnp.float32
                )
                attn = (both[:, :HD] / both[:, HD:]).astype(jnp.bfloat16)
                for j, col in enumerate(block):
                    out[:, col] = attn[j * part : (j + 1) * part]


def place_kernel(slots, groups, *refs):
    pieces, out, sem = refs[: len(slots)], refs[-2], refs[-1]
    width = pieces[0].shape[1]
    me = lax.axis_index("head")
    copies = []
    for index, (d, g) in enumerate(slots):
        at = pl.multiple_of((jnp.bitwise_xor(me, d) * groups + g) * width, width)
        copies.append(
            pltpu.make_async_copy(pieces[index], out.at[0, :, pl.ds(at, width)], sem.at[index])
        )
    for copy in copies:
        copy.start()
    for copy in copies:
        copy.wait()


def local(queries, keys, values, order, doc_lengths):
    rows = queries.shape[1]
    groups = keys.shape[2] // HD
    width = queries.shape[2] // groups
    shards = lax.axis_size("ctx")
    heads = lax.axis_size("head")
    sections = lax.axis_size("section")
    part = rows // heads
    smem = pl.BlockSpec(memory_space=pltpu.SMEM)
    vmem = pl.BlockSpec(memory_space=VMEM)
    anywhere = pl.BlockSpec(memory_space=pl.ANY)
    params = pltpu.CompilerParams(vmem_limit_bytes=VMEM_LIMIT)
    turn = sorted(range(heads), key=lambda d: (-bin(d).count("1"), d))

    def handed(value, step):
        pairs = [
            (c * sections + s, (c ^ step) * sections + (s + 1) % sections)
            for c in range(shards)
            for s in range(sections)
        ]
        return lax.ppermute(value, ("ctx", "section"), pairs)

    def passed(value, step):
        return lax.ppermute(value, "ctx", [(c, c ^ step) for c in range(shards)])

    def after(value, *others):
        return lax.optimization_barrier((value, *others))[0]

    rows_q = handed(queries, 0)
    bias = pl.pallas_call(
        bias_kernel,
        out_shape=jax.ShapeDtypeStruct((rows, rows * shards), jnp.float32),
        in_specs=[smem, vmem],
        out_specs=vmem,
        compiler_params=params,
        name="bias",
    )(doc_lengths, order.reshape(shards, rows))

    packed = [
        jnp.concatenate([kv[0, :, g * HD : (g + 1) * HD] for kv in (keys, values)], axis=1)
        for g in range(groups)
    ]
    stacked = jnp.stack(packed)
    step = shards // 2
    blocks = {step: [handed(block, step) for block in packed]}
    own = handed(after(stacked, bias), 0)
    while step > 1:
        step //= 2
        for other in sorted(blocks):
            blocks[other ^ step] = [passed(after(block, bias), step) for block in blocks[other]]
        blocks[step] = [handed(after(stacked, bias), step)]
    kvs = [
        [own] + [blocks[step][g % len(blocks[step])] for step in range(1, shards)]
        for g in range(groups)
    ]

    def attend(slots, *others):
        needed = [block for g in sorted({g for _, g in slots}) for block in kvs[g]]
        return pl.pallas_call(
            functools.partial(attend_kernel, LOG2E / HD**0.5, slots, shards),
            out_shape=[jax.ShapeDtypeStruct((part, width), jnp.bfloat16)] * len(slots),
            in_specs=[vmem] * (2 + len(needed)) + [anywhere] * len(others),
            out_specs=[vmem] * len(slots),
            compiler_params=params,
            cost_estimate=pl.CostEstimate(
                flops=6 * part * width * rows * shards * len(slots),
                bytes_accessed=4 * part * width * len(slots),
                transcendentals=rows * shards * part * width // HD * len(slots),
            ),
            name="attend",
        )(rows_q, bias, *needed, *others)

    arrived = {}
    last = []
    for g in range(groups):
        parts = ((3,), (1, 2)) if g + 1 < groups else ((3, 1, 2),)
        for index, partners in enumerate(parts):
            slots = [(d, g) for d in partners]
            pieces = attend(slots, *last)
            last = [pieces[-1]]
            for (d, _), piece in zip(slots, pieces):
                if g and d == 2:
                    piece = after(piece, arrived[3, g - 1])
                arrived[d, g] = lax.ppermute(piece, "head", [(h, h ^ d) for h in range(heads)])
    slots = [(0, g) for g in range(groups)]
    for slot, piece in zip(slots, attend(slots, *last)):
        arrived[slot] = piece

    final = groups - 1
    out = []
    for slots in [[(d, g) for g in range(final) for d in turn[:-1]] + [(0, g) for g in range(groups)], [(turn[0], final)], [(d, final) for d in turn[1:-1]]]:
        out = [
            pl.pallas_call(
                functools.partial(place_kernel, slots, groups),
                out_shape=jax.ShapeDtypeStruct((1, part, heads * groups * width), jnp.bfloat16),
                in_specs=[anywhere] * (len(slots) + len(out)),
                out_specs=anywhere,
                scratch_shapes=[pltpu.SemaphoreType.DMA((len(slots),))],
                input_output_aliases={len(slots): 0} if out else {},
                compiler_params=params,
                name="place",
            )(*[arrived[slot] for slot in slots], *out)
        ]
    return out[0]


def solution(mesh):
    in_specs = (
        P("section", "ctx", "head"),
        P("section", "ctx", "head"),
        P("section", "ctx", "head"),
        P(),
        P(),
    )
    out_specs = P("section", ("ctx", "head"), None)
    return jax.shard_map(local, mesh=mesh, in_specs=in_specs, out_specs=out_specs, check_vma=False)
```

```python
import functools

import jax
import jax.numpy as jnp
from jax import lax
from jax.experimental import pallas as pl
from jax.experimental.pallas import tpu as pltpu
from jax.sharding import PartitionSpec as P

HD = 128
LOG2E = 1.4426950408889634
VMEM = pltpu.VMEM
VMEM_LIMIT = 48 * 1024 * 1024
BLOCK = 8


def bias_kernel(lengths, order, *refs):
    bias = refs[-1]
    shards, rows = order.shape
    c = lax.axis_index("ctx")
    pos = order[pl.ds(c, 1), :]
    lo = jnp.zeros_like(pos)
    start = jnp.int32(0)
    for n in range(lengths.shape[0]):
        lo = jnp.where(pos >= start, start, lo)
        start = start + lengths[n]
    square = (rows, rows)
    pos_rows = jnp.transpose(jnp.broadcast_to(pos.astype(jnp.float32), square))
    lo_rows = jnp.transpose(jnp.broadcast_to(lo.astype(jnp.float32), square))

    for step in range(shards):
        key_pos = order[pl.ds(jnp.bitwise_xor(c, step), 1), :].astype(jnp.float32)
        seen = (key_pos >= lo_rows) & (key_pos <= pos_rows)
        bias[:, step * rows : (step + 1) * rows] = jnp.where(seen, 0.0, -jnp.inf)


def attend_kernel(scale, slots, pieces, q, bias, *refs):
    outs = refs[-len(slots) :]
    part, width = outs[0].shape
    heads = width // HD
    me = lax.axis_index("head")
    for index, group in enumerate(sorted({group for _, group in slots})):
        kvs = refs[index * pieces : (index + 1) * pieces]
        kvs = [kv[group] if len(kv.shape) == 3 else kv[...] for kv in kvs]
        keys = jnp.concatenate([kv[:, :HD] for kv in kvs], axis=0)
        vals = jnp.concatenate([kv[:, HD:] for kv in kvs], axis=0)
        vals = jnp.concatenate([vals, jnp.ones_like(vals)], axis=1)
        for d, out in [(d, out) for (d, g), out in zip(slots, outs) if g == group]:
            rows = pl.ds(pl.multiple_of(jnp.bitwise_xor(me, d) * part, part), part)
            seen = bias[rows, :][None]
            for first in range(0, heads, BLOCK):
                block = [slice(j * HD, (j + 1) * HD) for j in range(first, min(first + BLOCK, heads))]
                shift = group * width
                stacked = jnp.concatenate(
                    [q[0, rows, shift + col.start : shift + col.stop] for col in block], axis=0
                )
                score = lax.dot_general(
                    stacked, keys, (((1,), (1,)), ((), ())), preferred_element_type=jnp.float32
                )
                score = score.reshape(len(block), part, -1) + seen
                top = jnp.max(score, axis=2, keepdims=True)
                weight = jnp.exp2((score - top) * scale).astype(jnp.bfloat16)
                both = jnp.dot(
                    weight.reshape(len(block) * part, -1), vals, preferred_element_type=jnp.float32
                )
                attn = (both[:, :HD] / both[:, HD:]).astype(jnp.bfloat16)
                for j, col in enumerate(block):
                    out[:, col] = attn[j * part : (j + 1) * part]


def place_kernel(slots, groups, *refs):
    pieces, out, sem = refs[: len(slots)], refs[-2], refs[-1]
    width = pieces[0].shape[1]
    me = lax.axis_index("head")
    copies = []
    for index, (d, g) in enumerate(slots):
        at = pl.multiple_of((jnp.bitwise_xor(me, d) * groups + g) * width, width)
        copies.append(
            pltpu.make_async_copy(pieces[index], out.at[0, :, pl.ds(at, width)], sem.at[index])
        )
    for copy in copies:
        copy.start()
    for copy in copies:
        copy.wait()


def local(queries, keys, values, order, doc_lengths):
    rows = queries.shape[1]
    groups = keys.shape[2] // HD
    width = queries.shape[2] // groups
    shards = lax.axis_size("ctx")
    heads = lax.axis_size("head")
    sections = lax.axis_size("section")
    part = rows // heads
    smem = pl.BlockSpec(memory_space=pltpu.SMEM)
    vmem = pl.BlockSpec(memory_space=VMEM)
    anywhere = pl.BlockSpec(memory_space=pl.ANY)
    params = pltpu.CompilerParams(vmem_limit_bytes=VMEM_LIMIT)
    turn = sorted(range(heads), key=lambda d: (-bin(d).count("1"), d))

    def handed(value, step):
        pairs = [
            (c * sections + s, (c ^ step) * sections + (s + 1) % sections)
            for c in range(shards)
            for s in range(sections)
        ]
        return lax.ppermute(value, ("ctx", "section"), pairs)

    def passed(value, step):
        return lax.ppermute(value, "ctx", [(c, c ^ step) for c in range(shards)])

    def after(value, *others):
        return lax.optimization_barrier((value, *others))[0]

    rows_q = handed(queries, 0)
    bias = pl.pallas_call(
        bias_kernel,
        out_shape=jax.ShapeDtypeStruct((rows, rows * shards), jnp.float32),
        in_specs=[smem, vmem],
        out_specs=vmem,
        compiler_params=params,
        name="bias",
    )(doc_lengths, order.reshape(shards, rows))

    packed = [
        jnp.concatenate([kv[0, :, g * HD : (g + 1) * HD] for kv in (keys, values)], axis=1)
        for g in range(groups)
    ]
    stacked = jnp.stack(packed)
    step = shards // 2
    blocks = {step: [handed(block, step) for block in packed]}
    own = handed(after(stacked, bias), 0)
    while step > 1:
        step //= 2
        for other in sorted(blocks):
            blocks[other ^ step] = [passed(after(block, bias), step) for block in blocks[other]]
        blocks[step] = [handed(stacked, step)]
    kvs = [
        [own] + [blocks[step][g % len(blocks[step])] for step in range(1, shards)]
        for g in range(groups)
    ]

    def attend(slots, *others):
        needed = [block for g in sorted({g for _, g in slots}) for block in kvs[g]]
        return pl.pallas_call(
            functools.partial(attend_kernel, LOG2E / HD**0.5, slots, shards),
            out_shape=[jax.ShapeDtypeStruct((part, width), jnp.bfloat16)] * len(slots),
            in_specs=[vmem] * (2 + len(needed)) + [anywhere] * len(others),
            out_specs=[vmem] * len(slots),
            compiler_params=params,
            cost_estimate=pl.CostEstimate(
                flops=4 * part * width * rows * shards * len(slots),
                bytes_accessed=4 * part * width * len(slots),
                transcendentals=rows * shards * part * width // HD * len(slots),
            ),
            name="attend",
        )(rows_q, bias, *needed, *others)

    arrived = {}
    last = []
    for g in range(groups):
        parts = ((3,), (1, 2)) if g + 1 < groups else ((3, 1, 2),)
        for index, partners in enumerate(parts):
            for d in [(3,)][index] if g else ():
                last.append(arrived[d, g - 1])
            slots = [(d, g) for d in partners]
            pieces = attend(slots, *last)
            last = [pieces[-1]]
            for (d, _), piece in zip(slots, pieces):
                arrived[d, g] = lax.ppermute(piece, "head", [(h, h ^ d) for h in range(heads)])
    slots = [(0, g) for g in range(groups)]
    for slot, piece in zip(slots, attend(slots, *last)):
        arrived[slot] = piece

    final = groups - 1
    out = []
    for slots in [[(d, g) for g in range(final) for d in turn[:-1]] + [(0, g) for g in range(groups)], [(turn[0], final)], [(d, final) for d in turn[1:-1]]]:
        out = [
            pl.pallas_call(
                functools.partial(place_kernel, slots, groups),
                out_shape=jax.ShapeDtypeStruct((1, part, heads * groups * width), jnp.bfloat16),
                in_specs=[anywhere] * (len(slots) + len(out)),
                out_specs=anywhere,
                scratch_shapes=[pltpu.SemaphoreType.DMA((len(slots),))],
                input_output_aliases={len(slots): 0} if out else {},
                compiler_params=params,
                name="place",
            )(*[arrived[slot] for slot in slots], *out)
        ]
    return out[0]


def solution(mesh):
    in_specs = (
        P("section", "ctx", "head"),
        P("section", "ctx", "head"),
        P("section", "ctx", "head"),
        P(),
        P(),
    )
    out_specs = P("section", ("ctx", "head"), None)
    return jax.shard_map(local, mesh=mesh, in_specs=in_specs, out_specs=out_specs, check_vma=False)
```

```python
import functools

import jax
import jax.numpy as jnp
from jax import lax
from jax.experimental import pallas as pl
from jax.experimental.pallas import tpu as pltpu
from jax.sharding import PartitionSpec as P

HD = 128
LOG2E = 1.4426950408889634
VMEM = pltpu.VMEM
VMEM_LIMIT = 48 * 1024 * 1024
BLOCK = 8


def bias_kernel(lengths, order, *refs):
    bias = refs[-1]
    shards, rows = order.shape
    c = lax.axis_index("ctx")
    pos = order[pl.ds(c, 1), :]
    lo = jnp.zeros_like(pos)
    start = jnp.int32(0)
    for n in range(lengths.shape[0]):
        lo = jnp.where(pos >= start, start, lo)
        start = start + lengths[n]
    square = (rows, rows)
    pos_rows = jnp.transpose(jnp.broadcast_to(pos.astype(jnp.float32), square))
    lo_rows = jnp.transpose(jnp.broadcast_to(lo.astype(jnp.float32), square))

    for step in range(shards):
        key_pos = order[pl.ds(jnp.bitwise_xor(c, step), 1), :].astype(jnp.float32)
        seen = (key_pos >= lo_rows) & (key_pos <= pos_rows)
        bias[:, step * rows : (step + 1) * rows] = jnp.where(seen, 0.0, -jnp.inf)


def attend_kernel(scale, slots, pieces, q, bias, *refs):
    outs = refs[-len(slots) :]
    part, width = outs[0].shape
    heads = width // HD
    me = lax.axis_index("head")
    for index, group in enumerate(sorted({group for _, group in slots})):
        kvs = refs[index * pieces : (index + 1) * pieces]
        kvs = [kv[group] if len(kv.shape) == 3 else kv[...] for kv in kvs]
        keys = jnp.concatenate([kv[:, :HD] for kv in kvs], axis=0)
        vals = jnp.concatenate([kv[:, HD:] for kv in kvs], axis=0)
        vals = jnp.concatenate([vals, jnp.ones_like(vals)], axis=1)
        for d, out in [(d, out) for (d, g), out in zip(slots, outs) if g == group]:
            rows = pl.ds(pl.multiple_of(jnp.bitwise_xor(me, d) * part, part), part)
            seen = bias[rows, :][None]
            for first in range(0, heads, BLOCK):
                block = [slice(j * HD, (j + 1) * HD) for j in range(first, min(first + BLOCK, heads))]
                shift = group * width
                stacked = jnp.concatenate(
                    [q[0, rows, shift + col.start : shift + col.stop] for col in block], axis=0
                )
                score = lax.dot_general(
                    stacked, keys, (((1,), (1,)), ((), ())), preferred_element_type=jnp.float32
                )
                score = score.reshape(len(block), part, -1) + seen
                top = jnp.max(score, axis=2, keepdims=True)
                weight = jnp.exp2((score - top) * scale).astype(jnp.bfloat16)
                both = jnp.dot(
                    weight.reshape(len(block) * part, -1), vals, preferred_element_type=jnp.float32
                )
                attn = (both[:, :HD] / both[:, HD:]).astype(jnp.bfloat16)
                for j, col in enumerate(block):
                    out[:, col] = attn[j * part : (j + 1) * part]


def place_kernel(slots, groups, *refs):
    pieces, out, sem = refs[: len(slots)], refs[-2], refs[-1]
    width = pieces[0].shape[1]
    me = lax.axis_index("head")
    copies = []
    for index, (d, g) in enumerate(slots):
        at = pl.multiple_of((jnp.bitwise_xor(me, d) * groups + g) * width, width)
        copies.append(
            pltpu.make_async_copy(pieces[index], out.at[0, :, pl.ds(at, width)], sem.at[index])
        )
    for copy in copies:
        copy.start()
    for copy in copies:
        copy.wait()


def local(queries, keys, values, order, doc_lengths):
    rows = queries.shape[1]
    groups = keys.shape[2] // HD
    width = queries.shape[2] // groups
    shards = lax.axis_size("ctx")
    heads = lax.axis_size("head")
    sections = lax.axis_size("section")
    part = rows // heads
    smem = pl.BlockSpec(memory_space=pltpu.SMEM)
    vmem = pl.BlockSpec(memory_space=VMEM)
    anywhere = pl.BlockSpec(memory_space=pl.ANY)
    params = pltpu.CompilerParams(vmem_limit_bytes=VMEM_LIMIT)
    turn = sorted(range(heads), key=lambda d: (-bin(d).count("1"), d))

    def handed(value, step):
        pairs = [
            (c * sections + s, (c ^ step) * sections + (s + 1) % sections)
            for c in range(shards)
            for s in range(sections)
        ]
        return lax.ppermute(value, ("ctx", "section"), pairs)

    def passed(value, step):
        return lax.ppermute(value, "ctx", [(c, c ^ step) for c in range(shards)])

    def after(value, *others):
        return lax.optimization_barrier((value, *others))[0]

    rows_q = handed(queries, 0)
    bias = pl.pallas_call(
        bias_kernel,
        out_shape=jax.ShapeDtypeStruct((rows, rows * shards), jnp.float32),
        in_specs=[smem, vmem],
        out_specs=vmem,
        compiler_params=params,
        name="bias",
    )(doc_lengths, order.reshape(shards, rows))

    packed = [
        jnp.concatenate([kv[0, :, g * HD : (g + 1) * HD] for kv in (keys, values)], axis=1)
        for g in range(groups)
    ]
    stacked = jnp.stack(packed)
    step = shards // 2
    blocks = {step: [handed(block, step) for block in packed]}
    own = handed(after(stacked, bias), 0)
    while step > 1:
        step //= 2
        for other in sorted(blocks):
            blocks[other ^ step] = [passed(after(block, bias), step) for block in blocks[other]]
        blocks[step] = [handed(stacked, step)]
    kvs = [
        [own] + [blocks[step][g % len(blocks[step])] for step in range(1, shards)]
        for g in range(groups)
    ]

    def attend(slots, *others):
        needed = [block for g in sorted({g for _, g in slots}) for block in kvs[g]]
        return pl.pallas_call(
            functools.partial(attend_kernel, LOG2E / HD**0.5, slots, shards),
            out_shape=[jax.ShapeDtypeStruct((part, width), jnp.bfloat16)] * len(slots),
            in_specs=[vmem] * (2 + len(needed)) + [anywhere] * len(others),
            out_specs=[vmem] * len(slots),
            compiler_params=params,
            cost_estimate=pl.CostEstimate(
                flops=4 * part * width * rows * shards * len(slots),
                bytes_accessed=4 * part * width * len(slots),
                transcendentals=rows * shards * part * width // HD * len(slots),
            ),
            name="attend",
        )(rows_q, bias, *needed, *others)

    arrived = {}
    last = []
    for g in range(groups):
        parts = ((3,), (1, 2)) if g + 1 < groups else ((3, 1, 2),)
        for index, partners in enumerate(parts):
            slots = [(d, g) for d in partners]
            pieces = attend(slots, *last)
            last = [pieces[-1]]
            for (d, _), piece in zip(slots, pieces):
                if g and d == 1:
                    piece = after(piece, arrived[3, g - 1])
                arrived[d, g] = lax.ppermute(piece, "head", [(h, h ^ d) for h in range(heads)])
    slots = [(0, g) for g in range(groups)]
    for slot, piece in zip(slots, attend(slots, *last)):
        arrived[slot] = piece

    final = groups - 1
    out = []
    for slots in [[(d, g) for g in range(final) for d in turn[:-1]] + [(0, g) for g in range(groups)], [(turn[0], final)], [(d, final) for d in turn[1:-1]]]:
        out = [
            pl.pallas_call(
                functools.partial(place_kernel, slots, groups),
                out_shape=jax.ShapeDtypeStruct((1, part, heads * groups * width), jnp.bfloat16),
                in_specs=[anywhere] * (len(slots) + len(out)),
                out_specs=anywhere,
                scratch_shapes=[pltpu.SemaphoreType.DMA((len(slots),))],
                input_output_aliases={len(slots): 0} if out else {},
                compiler_params=params,
                name="place",
            )(*[arrived[slot] for slot in slots], *out)
        ]
    return out[0]


def solution(mesh):
    in_specs = (
        P("section", "ctx", "head"),
        P("section", "ctx", "head"),
        P("section", "ctx", "head"),
        P(),
        P(),
    )
    out_specs = P("section", ("ctx", "head"), None)
    return jax.shard_map(local, mesh=mesh, in_specs=in_specs, out_specs=out_specs, check_vma=False)
```

```python
import functools

import jax
import jax.numpy as jnp
from jax import lax
from jax.experimental import pallas as pl
from jax.experimental.pallas import tpu as pltpu
from jax.sharding import PartitionSpec as P

HD = 128
LOG2E = 1.4426950408889634
VMEM = pltpu.VMEM
VMEM_LIMIT = 48 * 1024 * 1024
BLOCK = 8


def bias_kernel(lengths, order, *refs):
    bias = refs[-1]
    shards, rows = order.shape
    c = lax.axis_index("ctx")
    pos = order[pl.ds(c, 1), :]
    lo = jnp.zeros_like(pos)
    start = jnp.int32(0)
    for n in range(lengths.shape[0]):
        lo = jnp.where(pos >= start, start, lo)
        start = start + lengths[n]
    square = (rows, rows)
    pos_rows = jnp.transpose(jnp.broadcast_to(pos.astype(jnp.float32), square))
    lo_rows = jnp.transpose(jnp.broadcast_to(lo.astype(jnp.float32), square))

    for step in range(shards):
        key_pos = order[pl.ds(jnp.bitwise_xor(c, step), 1), :].astype(jnp.float32)
        seen = (key_pos >= lo_rows) & (key_pos <= pos_rows)
        bias[:, step * rows : (step + 1) * rows] = jnp.where(seen, 0.0, -jnp.inf)


def attend_kernel(scale, slots, pieces, q, bias, *refs):
    outs = refs[-len(slots) :]
    part, width = outs[0].shape
    heads = width // HD
    me = lax.axis_index("head")
    for index, group in enumerate(sorted({group for _, group in slots})):
        kvs = refs[index * pieces : (index + 1) * pieces]
        kvs = [kv[group] if len(kv.shape) == 3 else kv[...] for kv in kvs]
        keys = jnp.concatenate([kv[:, :HD] for kv in kvs], axis=0)
        vals = jnp.concatenate([kv[:, HD:] for kv in kvs], axis=0)
        vals = jnp.concatenate([vals, jnp.ones_like(vals)], axis=1)
        for d, out in [(d, out) for (d, g), out in zip(slots, outs) if g == group]:
            rows = pl.ds(pl.multiple_of(jnp.bitwise_xor(me, d) * part, part), part)
            seen = bias[rows, :][None]
            for first in range(0, heads, BLOCK):
                block = [slice(j * HD, (j + 1) * HD) for j in range(first, min(first + BLOCK, heads))]
                shift = group * width
                stacked = jnp.concatenate(
                    [q[0, rows, shift + col.start : shift + col.stop] for col in block], axis=0
                )
                score = lax.dot_general(
                    stacked, keys, (((1,), (1,)), ((), ())), preferred_element_type=jnp.float32
                )
                score = score.reshape(len(block), part, -1) + seen
                top = jnp.max(score, axis=2, keepdims=True)
                weight = jnp.exp2((score - top) * scale).astype(jnp.bfloat16)
                both = jnp.dot(
                    weight.reshape(len(block) * part, -1), vals, preferred_element_type=jnp.float32
                )
                attn = (both[:, :HD] / both[:, HD:]).astype(jnp.bfloat16)
                for j, col in enumerate(block):
                    out[:, col] = attn[j * part : (j + 1) * part]


def place_kernel(slots, groups, *refs):
    pieces, out, sem = refs[: len(slots)], refs[-2], refs[-1]
    width = pieces[0].shape[1]
    me = lax.axis_index("head")
    copies = []
    for index, (d, g) in enumerate(slots):
        at = pl.multiple_of((jnp.bitwise_xor(me, d) * groups + g) * width, width)
        copies.append(
            pltpu.make_async_copy(pieces[index], out.at[0, :, pl.ds(at, width)], sem.at[index])
        )
    for copy in copies:
        copy.start()
    for copy in copies:
        copy.wait()


def local(queries, keys, values, order, doc_lengths):
    rows = queries.shape[1]
    groups = keys.shape[2] // HD
    width = queries.shape[2] // groups
    shards = lax.axis_size("ctx")
    heads = lax.axis_size("head")
    sections = lax.axis_size("section")
    part = rows // heads
    smem = pl.BlockSpec(memory_space=pltpu.SMEM)
    vmem = pl.BlockSpec(memory_space=VMEM)
    anywhere = pl.BlockSpec(memory_space=pl.ANY)
    params = pltpu.CompilerParams(vmem_limit_bytes=VMEM_LIMIT)
    turn = sorted(range(heads), key=lambda d: (-bin(d).count("1"), d))

    def handed(value, step):
        pairs = [
            (c * sections + s, (c ^ step) * sections + (s + 1) % sections)
            for c in range(shards)
            for s in range(sections)
        ]
        return lax.ppermute(value, ("ctx", "section"), pairs)

    def passed(value, step):
        return lax.ppermute(value, "ctx", [(c, c ^ step) for c in range(shards)])

    def after(value, *others):
        return lax.optimization_barrier((value, *others))[0]

    rows_q = handed(queries, 0)
    bias = pl.pallas_call(
        bias_kernel,
        out_shape=jax.ShapeDtypeStruct((rows, rows * shards), jnp.float32),
        in_specs=[smem, vmem],
        out_specs=vmem,
        compiler_params=params,
        name="bias",
    )(doc_lengths, order.reshape(shards, rows))

    packed = [
        jnp.concatenate([kv[0, :, g * HD : (g + 1) * HD] for kv in (keys, values)], axis=1)
        for g in range(groups)
    ]
    stacked = jnp.stack(packed)
    step = shards // 2
    blocks = {step: [handed(block, step) for block in packed]}
    own = handed(after(stacked, bias), 0)
    while step > 1:
        step //= 2
        for other in sorted(blocks):
            blocks[other ^ step] = [passed(after(block, bias), step) for block in blocks[other]]
        blocks[step] = [handed(stacked, step)]
    kvs = [
        [own] + [blocks[step][g % len(blocks[step])] for step in range(1, shards)]
        for g in range(groups)
    ]

    def attend(slots, *others):
        needed = [block for g in sorted({g for _, g in slots}) for block in kvs[g]]
        return pl.pallas_call(
            functools.partial(attend_kernel, LOG2E / HD**0.5, slots, shards),
            out_shape=[jax.ShapeDtypeStruct((part, width), jnp.bfloat16)] * len(slots),
            in_specs=[vmem] * (2 + len(needed)) + [anywhere] * len(others),
            out_specs=[vmem] * len(slots),
            compiler_params=params,
            cost_estimate=pl.CostEstimate(
                flops=4 * part * width * rows * shards * len(slots),
                bytes_accessed=4 * part * width * len(slots),
                transcendentals=rows * shards * part * width // HD * len(slots),
            ),
            name="attend",
        )(rows_q, bias, *needed, *others)

    arrived = {}
    last = []
    for g in range(groups):
        parts = ((3, 1, 2),) if g + 1 < groups else ((3, 1, 2),)
        for index, partners in enumerate(parts):
            slots = [(d, g) for d in partners]
            pieces = attend(slots, *last)
            last = [pieces[-1]]
            for (d, _), piece in zip(slots, pieces):
                if g and d == 1:
                    piece = after(piece, arrived[3, g - 1])
                arrived[d, g] = lax.ppermute(piece, "head", [(h, h ^ d) for h in range(heads)])
    slots = [(0, g) for g in range(groups)]
    for slot, piece in zip(slots, attend(slots, *last)):
        arrived[slot] = piece

    final = groups - 1
    out = []
    for slots in [[(d, g) for g in range(final) for d in turn[:-1]] + [(0, g) for g in range(groups)], [(turn[0], final)], [(d, final) for d in turn[1:-1]]]:
        out = [
            pl.pallas_call(
                functools.partial(place_kernel, slots, groups),
                out_shape=jax.ShapeDtypeStruct((1, part, heads * groups * width), jnp.bfloat16),
                in_specs=[anywhere] * (len(slots) + len(out)),
                out_specs=anywhere,
                scratch_shapes=[pltpu.SemaphoreType.DMA((len(slots),))],
                input_output_aliases={len(slots): 0} if out else {},
                compiler_params=params,
                name="place",
            )(*[arrived[slot] for slot in slots], *out)
        ]
    return out[0]


def solution(mesh):
    in_specs = (
        P("section", "ctx", "head"),
        P("section", "ctx", "head"),
        P("section", "ctx", "head"),
        P(),
        P(),
    )
    out_specs = P("section", ("ctx", "head"), None)
    return jax.shard_map(local, mesh=mesh, in_specs=in_specs, out_specs=out_specs, check_vma=False)
```

```python
import functools

import jax
import jax.numpy as jnp
from jax import lax
from jax.experimental import pallas as pl
from jax.experimental.pallas import tpu as pltpu
from jax.sharding import PartitionSpec as P

HD = 128
LOG2E = 1.4426950408889634
VMEM = pltpu.VMEM
VMEM_LIMIT = 48 * 1024 * 1024
BLOCK = 8


def bias_kernel(lengths, order, *refs):
    bias = refs[-1]
    shards, rows = order.shape
    c = lax.axis_index("ctx")
    pos = order[pl.ds(c, 1), :]
    lo = jnp.zeros_like(pos)
    start = jnp.int32(0)
    for n in range(lengths.shape[0]):
        lo = jnp.where(pos >= start, start, lo)
        start = start + lengths[n]
    square = (rows, rows)
    pos_rows = jnp.transpose(jnp.broadcast_to(pos.astype(jnp.float32), square))
    lo_rows = jnp.transpose(jnp.broadcast_to(lo.astype(jnp.float32), square))

    for step in range(shards):
        key_pos = order[pl.ds(jnp.bitwise_xor(c, step), 1), :].astype(jnp.float32)
        seen = (key_pos >= lo_rows) & (key_pos <= pos_rows)
        bias[:, step * rows : (step + 1) * rows] = jnp.where(seen, 0.0, -jnp.inf)


def attend_kernel(scale, slots, pieces, q, bias, *refs):
    outs = refs[-len(slots) :]
    part, width = outs[0].shape
    heads = width // HD
    me = lax.axis_index("head")
    for index, group in enumerate(sorted({group for _, group in slots})):
        kvs = refs[index * pieces : (index + 1) * pieces]
        kvs = [kv[group] if len(kv.shape) == 3 else kv[...] for kv in kvs]
        keys = jnp.concatenate([kv[:, :HD] for kv in kvs], axis=0)
        vals = jnp.concatenate([kv[:, HD:] for kv in kvs], axis=0)
        vals = jnp.concatenate([vals, jnp.ones_like(vals)], axis=1)
        for d, out in [(d, out) for (d, g), out in zip(slots, outs) if g == group]:
            rows = pl.ds(pl.multiple_of(jnp.bitwise_xor(me, d) * part, part), part)
            seen = bias[rows, :][None]
            for first in range(0, heads, BLOCK):
                block = [slice(j * HD, (j + 1) * HD) for j in range(first, min(first + BLOCK, heads))]
                shift = group * width
                stacked = jnp.concatenate(
                    [q[0, rows, shift + col.start : shift + col.stop] for col in block], axis=0
                )
                score = lax.dot_general(
                    stacked, keys, (((1,), (1,)), ((), ())), preferred_element_type=jnp.float32
                )
                score = score.reshape(len(block), part, -1) + seen
                top = jnp.max(score, axis=2, keepdims=True)
                weight = jnp.exp2((score - top) * scale).astype(jnp.bfloat16)
                both = jnp.dot(
                    weight.reshape(len(block) * part, -1), vals, preferred_element_type=jnp.float32
                )
                attn = (both[:, :HD] / both[:, HD:]).astype(jnp.bfloat16)
                for j, col in enumerate(block):
                    out[:, col] = attn[j * part : (j + 1) * part]


def place_kernel(slots, groups, *refs):
    pieces, out, sem = refs[: len(slots)], refs[-2], refs[-1]
    width = pieces[0].shape[1]
    me = lax.axis_index("head")
    copies = []
    for index, (d, g) in enumerate(slots):
        at = pl.multiple_of((jnp.bitwise_xor(me, d) * groups + g) * width, width)
        copies.append(
            pltpu.make_async_copy(pieces[index], out.at[0, :, pl.ds(at, width)], sem.at[index])
        )
    for copy in copies:
        copy.start()
    for copy in copies:
        copy.wait()


def local(queries, keys, values, order, doc_lengths):
    rows = queries.shape[1]
    groups = keys.shape[2] // HD
    width = queries.shape[2] // groups
    shards = lax.axis_size("ctx")
    heads = lax.axis_size("head")
    sections = lax.axis_size("section")
    part = rows // heads
    smem = pl.BlockSpec(memory_space=pltpu.SMEM)
    vmem = pl.BlockSpec(memory_space=VMEM)
    anywhere = pl.BlockSpec(memory_space=pl.ANY)
    params = pltpu.CompilerParams(vmem_limit_bytes=VMEM_LIMIT)
    turn = sorted(range(heads), key=lambda d: (-bin(d).count("1"), d))

    def handed(value, step):
        pairs = [
            (c * sections + s, (c ^ step) * sections + (s + 1) % sections)
            for c in range(shards)
            for s in range(sections)
        ]
        return lax.ppermute(value, ("ctx", "section"), pairs)

    def passed(value, step):
        return lax.ppermute(value, "ctx", [(c, c ^ step) for c in range(shards)])

    def after(value, *others):
        return lax.optimization_barrier((value, *others))[0]

    rows_q = handed(queries, 0)
    bias = pl.pallas_call(
        bias_kernel,
        out_shape=jax.ShapeDtypeStruct((rows, rows * shards), jnp.float32),
        in_specs=[smem, vmem, anywhere],
        out_specs=vmem,
        compiler_params=params,
        name="bias",
    )(doc_lengths, order.reshape(shards, rows), rows_q)

    packed = [
        jnp.concatenate([kv[0, :, g * HD : (g + 1) * HD] for kv in (keys, values)], axis=1)
        for g in range(groups)
    ]
    stacked = jnp.stack(packed)
    step = shards // 2
    blocks = {step: [handed(block, step) for block in packed]}
    own = handed(stacked, 0)
    while step > 1:
        step //= 2
        for other in sorted(blocks):
            ahead = [handed(packed[0], other ^ step)] if len(blocks[other]) > 1 else []
            blocks[other ^ step] = ahead + [
                passed(after(block, bias), step) for block in blocks[other][len(ahead) :]
            ]
        blocks[step] = [handed(stacked, step)]
    kvs = [
        [own] + [blocks[step][g % len(blocks[step])] for step in range(1, shards)]
        for g in range(groups)
    ]

    def attend(slots, *others):
        needed = [block for g in sorted({g for _, g in slots}) for block in kvs[g]]
        return pl.pallas_call(
            functools.partial(attend_kernel, LOG2E / HD**0.5, slots, shards),
            out_shape=[jax.ShapeDtypeStruct((part, width), jnp.bfloat16)] * len(slots),
            in_specs=[vmem] * (2 + len(needed)) + [anywhere] * len(others),
            out_specs=[vmem] * len(slots),
            compiler_params=params,
            cost_estimate=pl.CostEstimate(
                flops=4 * part * width * rows * shards * len(slots),
                bytes_accessed=4 * part * width * len(slots),
                transcendentals=rows * shards * part * width // HD * len(slots),
            ),
            name="attend",
        )(rows_q, bias, *needed, *others)

    arrived = {}
    last = []
    for g in range(groups):
        parts = ((3,), (1, 2)) if g + 1 < groups else ((3, 1, 2),)
        for index, partners in enumerate(parts):
            slots = [(d, g) for d in partners]
            pieces = attend(slots, *last)
            last = [pieces[-1]]
            for (d, _), piece in zip(slots, pieces):
                if g and d == 1:
                    piece = after(piece, arrived[3, g - 1])
                arrived[d, g] = lax.ppermute(piece, "head", [(h, h ^ d) for h in range(heads)])
    slots = [(0, g) for g in range(groups)]
    for slot, piece in zip(slots, attend(slots, *last)):
        arrived[slot] = piece

    final = groups - 1
    out = []
    for slots in [[(d, g) for g in range(final) for d in turn[:-1]] + [(0, g) for g in range(groups)], [(turn[0], final)], [(d, final) for d in turn[1:-1]]]:
        out = [
            pl.pallas_call(
                functools.partial(place_kernel, slots, groups),
                out_shape=jax.ShapeDtypeStruct((1, part, heads * groups * width), jnp.bfloat16),
                in_specs=[anywhere] * (len(slots) + len(out)),
                out_specs=anywhere,
                scratch_shapes=[pltpu.SemaphoreType.DMA((len(slots),))],
                input_output_aliases={len(slots): 0} if out else {},
                compiler_params=params,
                name="place",
            )(*[arrived[slot] for slot in slots], *out)
        ]
    return out[0]


def solution(mesh):
    in_specs = (
        P("section", "ctx", "head"),
        P("section", "ctx", "head"),
        P("section", "ctx", "head"),
        P(),
        P(),
    )
    out_specs = P("section", ("ctx", "head"), None)
    return jax.shard_map(local, mesh=mesh, in_specs=in_specs, out_specs=out_specs, check_vma=False)
```

```python
import functools

import jax
import jax.numpy as jnp
from jax import lax
from jax.experimental import pallas as pl
from jax.experimental.pallas import tpu as pltpu
from jax.sharding import PartitionSpec as P

HD = 128
LOG2E = 1.4426950408889634
VMEM = pltpu.VMEM
VMEM_LIMIT = 48 * 1024 * 1024
BLOCK = 4


def bias_kernel(lengths, order, *refs):
    bias = refs[-1]
    shards, rows = order.shape
    c = lax.axis_index("ctx")
    pos = order[pl.ds(c, 1), :]
    lo = jnp.zeros_like(pos)
    start = jnp.int32(0)
    for n in range(lengths.shape[0]):
        lo = jnp.where(pos >= start, start, lo)
        start = start + lengths[n]
    square = (rows, rows)
    pos_rows = jnp.transpose(jnp.broadcast_to(pos.astype(jnp.float32), square))
    lo_rows = jnp.transpose(jnp.broadcast_to(lo.astype(jnp.float32), square))

    for step in range(shards):
        key_pos = order[pl.ds(jnp.bitwise_xor(c, step), 1), :].astype(jnp.float32)
        seen = (key_pos >= lo_rows) & (key_pos <= pos_rows)
        bias[:, step * rows : (step + 1) * rows] = jnp.where(seen, 0.0, -jnp.inf)


def attend_kernel(scale, slots, pieces, q, bias, *refs):
    outs = refs[-len(slots) :]
    part, width = outs[0].shape
    heads = width // HD
    me = lax.axis_index("head")
    for index, group in enumerate(sorted({group for _, group in slots})):
        kvs = refs[index * pieces : (index + 1) * pieces]
        kvs = [kv[group] if len(kv.shape) == 3 else kv[...] for kv in kvs]
        keys = jnp.concatenate([kv[:, :HD] for kv in kvs], axis=0)
        vals = jnp.concatenate([kv[:, HD:] for kv in kvs], axis=0)
        vals = jnp.concatenate([vals, jnp.ones_like(vals)], axis=1)
        for d, out in [(d, out) for (d, g), out in zip(slots, outs) if g == group]:
            rows = pl.ds(pl.multiple_of(jnp.bitwise_xor(me, d) * part, part), part)
            seen = bias[rows, :][None]
            for first in range(0, heads, BLOCK):
                block = [slice(j * HD, (j + 1) * HD) for j in range(first, min(first + BLOCK, heads))]
                shift = group * width
                stacked = jnp.concatenate(
                    [q[0, rows, shift + col.start : shift + col.stop] for col in block], axis=0
                )
                score = lax.dot_general(
                    stacked, keys, (((1,), (1,)), ((), ())), preferred_element_type=jnp.float32
                )
                score = score.reshape(len(block), part, -1) + seen
                top = jnp.max(score, axis=2, keepdims=True)
                weight = jnp.exp2((score - top) * scale).astype(jnp.bfloat16)
                both = jnp.dot(
                    weight.reshape(len(block) * part, -1), vals, preferred_element_type=jnp.float32
                )
                attn = (both[:, :HD] / both[:, HD:]).astype(jnp.bfloat16)
                for j, col in enumerate(block):
                    out[:, col] = attn[j * part : (j + 1) * part]


def place_kernel(slots, groups, *refs):
    pieces, out, sem = refs[: len(slots)], refs[-2], refs[-1]
    width = pieces[0].shape[1]
    me = lax.axis_index("head")
    copies = []
    for index, (d, g) in enumerate(slots):
        at = pl.multiple_of((jnp.bitwise_xor(me, d) * groups + g) * width, width)
        copies.append(
            pltpu.make_async_copy(pieces[index], out.at[0, :, pl.ds(at, width)], sem.at[index])
        )
    for copy in copies:
        copy.start()
    for copy in copies:
        copy.wait()


def local(queries, keys, values, order, doc_lengths):
    rows = queries.shape[1]
    groups = keys.shape[2] // HD
    width = queries.shape[2] // groups
    shards = lax.axis_size("ctx")
    heads = lax.axis_size("head")
    sections = lax.axis_size("section")
    part = rows // heads
    smem = pl.BlockSpec(memory_space=pltpu.SMEM)
    vmem = pl.BlockSpec(memory_space=VMEM)
    anywhere = pl.BlockSpec(memory_space=pl.ANY)
    params = pltpu.CompilerParams(vmem_limit_bytes=VMEM_LIMIT)
    turn = sorted(range(heads), key=lambda d: (-bin(d).count("1"), d))

    def handed(value, step):
        pairs = [
            (c * sections + s, (c ^ step) * sections + (s + 1) % sections)
            for c in range(shards)
            for s in range(sections)
        ]
        return lax.ppermute(value, ("ctx", "section"), pairs)

    def passed(value, step):
        return lax.ppermute(value, "ctx", [(c, c ^ step) for c in range(shards)])

    def after(value, *others):
        return lax.optimization_barrier((value, *others))[0]

    rows_q = handed(queries, 0)
    bias = pl.pallas_call(
        bias_kernel,
        out_shape=jax.ShapeDtypeStruct((rows, rows * shards), jnp.float32),
        in_specs=[smem, vmem],
        out_specs=vmem,
        compiler_params=params,
        name="bias",
    )(doc_lengths, order.reshape(shards, rows))

    packed = [
        jnp.concatenate([kv[0, :, g * HD : (g + 1) * HD] for kv in (keys, values)], axis=1)
        for g in range(groups)
    ]
    stacked = jnp.stack(packed)
    step = shards // 2
    blocks = {step: [handed(block, step) for block in packed]}
    own = handed(after(stacked, bias), 0)
    while step > 1:
        step //= 2
        for other in sorted(blocks):
            blocks[other ^ step] = [passed(after(block, bias), step) for block in blocks[other]]
        blocks[step] = [handed(stacked, step)]
    kvs = [
        [own] + [blocks[step][g % len(blocks[step])] for step in range(1, shards)]
        for g in range(groups)
    ]

    def attend(slots, *others):
        needed = [block for g in sorted({g for _, g in slots}) for block in kvs[g]]
        return pl.pallas_call(
            functools.partial(attend_kernel, LOG2E / HD**0.5, slots, shards),
            out_shape=[jax.ShapeDtypeStruct((part, width), jnp.bfloat16)] * len(slots),
            in_specs=[vmem] * (2 + len(needed)) + [anywhere] * len(others),
            out_specs=[vmem] * len(slots),
            compiler_params=params,
            cost_estimate=pl.CostEstimate(
                flops=4 * part * width * rows * shards * len(slots),
                bytes_accessed=4 * part * width * len(slots),
                transcendentals=rows * shards * part * width // HD * len(slots),
            ),
            name="attend",
        )(rows_q, bias, *needed, *others)

    arrived = {}
    last = []
    for g in range(groups):
        parts = ((3,), (1, 2)) if g + 1 < groups else ((3, 1, 2),)
        for index, partners in enumerate(parts):
            slots = [(d, g) for d in partners]
            pieces = attend(slots, *last)
            last = [pieces[-1]]
            for (d, _), piece in zip(slots, pieces):
                if g and d == 1:
                    piece = after(piece, arrived[3, g - 1])
                arrived[d, g] = lax.ppermute(piece, "head", [(h, h ^ d) for h in range(heads)])
    slots = [(0, g) for g in range(groups)]
    for slot, piece in zip(slots, attend(slots, *last)):
        arrived[slot] = piece

    final = groups - 1
    out = []
    for slots in [[(d, g) for g in range(final) for d in turn[:-1]] + [(0, g) for g in range(groups)], [(turn[0], final)], [(d, final) for d in turn[1:-1]]]:
        out = [
            pl.pallas_call(
                functools.partial(place_kernel, slots, groups),
                out_shape=jax.ShapeDtypeStruct((1, part, heads * groups * width), jnp.bfloat16),
                in_specs=[anywhere] * (len(slots) + len(out)),
                out_specs=anywhere,
                scratch_shapes=[pltpu.SemaphoreType.DMA((len(slots),))],
                input_output_aliases={len(slots): 0} if out else {},
                compiler_params=params,
                name="place",
            )(*[arrived[slot] for slot in slots], *out)
        ]
    return out[0]


def solution(mesh):
    in_specs = (
        P("section", "ctx", "head"),
        P("section", "ctx", "head"),
        P("section", "ctx", "head"),
        P(),
        P(),
    )
    out_specs = P("section", ("ctx", "head"), None)
    return jax.shard_map(local, mesh=mesh, in_specs=in_specs, out_specs=out_specs, check_vma=False)
```
